32 devices in a mesh: groups: 2 (over y), lon: 16 (over z, x, core).
Axes of the slice: x: 2, y: 2, z: 4, core: 2. Of those that a mesh axis runs over, the one named last changes fastest.
Arguments:
- celerity: float32 [512, 2048], P('lon'), may hold values from 0.1 to 0.45
- station_tile: int32 [65536, 1], P(('groups', 'lon')), parts along dimension 0, may hold values from 0 to 15; in each aligned block of 2048 rows (0 to 2047, 2048 to 4095, ...) at most 256 rows name the same one
- station_block: int32 [65536], P(('groups', 'lon')), parts along dimension 0, may hold values from 0 to 511
- footprint: bfloat16 [65536, 128], P(('groups', 'lon')), parts along dimension 0, may hold values from 0 to 1
- misfit: bfloat16 [8, 65536], P(None, ('groups', 'lon')), parts along dimension 1, may hold values from -1.1953125 to 1.1953125
- segment_block: int32 [1024], P('lon'), may hold values from 0 to 511
- segment_fault: int32 [1024], P('lon'), may hold values from 0 to 63
- green_uplift: bfloat16 [1024, 256], P('lon'), may hold values from -0.5 to 0.5
Outputs:
- adjoint: float32 [1024, 2048], P(('groups', 'lon')), parts along dimension 0
- gradient: float32 [128, 64], P(('groups', 'lon')), parts along dimension 0
The draws below stay inside these ranges and needn't reach their ends.
There are 2 independent parts, one for each index of `groups`. The reference program is written for one: setup_inputs(seed, part) draws one part's arguments, and reference() takes and returns one part's arrays. A program takes and returns all parts, laid end to end along the dimension named above; an argument that names none is the same for every part. Nothing has to cross between parts.
Inputs may be any that keep to these rules, and one draw needn't show every extreme that they name: `station_tile`: in each aligned block of the 2048 observations of one device, no tile is named more than 256 times, a bound that some block reaches.
All inputs are finite; a program needn't handle non-finite values.
Results may differ from the reference program's by a relative error of at most 0.0003.
Values may be sent and summed in bfloat16 or wider, within the bound.
A program may use at most 64 MiB of HBM per device.

```python
import math
import jax
import jax.numpy as jnp
import numpy as np
from jax import lax

CLON = 32
NLAT = 2048
OBS_DEV = 2048
SEG_DEV = 64
STEPS = 8
NWIN = 32
NLON = 512
BLK = 512
CAP = 256
OBS_TOTAL = 32768
SEG_TOTAL = 1024
SUBF = 64
N_LON = 16


def place_ends(values, rng, least, top_value):
    spot = [jax.random.randint(jax.random.fold_in(rng, axis), (), 0, length) for axis, length in enumerate(values.shape)]
    longest = values.shape.index(max(values.shape))
    next_to = spot[:longest] + [(spot[longest] + 1) % values.shape[longest]] + spot[longest + 1:]
    return values.at[tuple(spot)].set(least).at[tuple(next_to)].set(top_value)


def block_levels(rng, dims, shards, low, largest):
    loudness = 1.0
    for axis_at, shards_of in shards:
        draws = jax.random.uniform(jax.random.fold_in(jax.random.fold_in(rng, 6), axis_at), (shards_of,), jnp.float32, low / len(shards), largest / len(shards))
        loudness = loudness * jnp.repeat(jnp.exp(draws), dims[axis_at] // shards_of).reshape((-1,) + (1,) * (len(dims) - 1 - axis_at))
    return loudness


def deal_out(rng, own, number, rows, count, top, limit, lean):
    order = jax.random.permutation(rng, count)
    crowded, ordinary = load_shares(count, rows * top, limit, lean, True), load_shares(count, rows * top, limit, lean, False)
    places = jnp.arange(count)

    def named(lengths, rotation):
        used = int((lengths > 0).sum())
        fixed = max(1, used // 4)
        passed = fixed + (places - fixed + rotation * (used - fixed)) % max(1, count - fixed)
        return jnp.zeros((count,), jnp.int32).at[order[jnp.where(places < fixed, places, passed)]].set(jnp.asarray(lengths, jnp.int32))

    lengths = jnp.where(number % 4 == 0, named(crowded, number // 4), named(ordinary, number - number // 4 - 1))
    mixed = jax.random.permutation(jax.random.fold_in(own, 3), count)
    giver, sink = mixed[0:count // 2 * 2:2], mixed[1:count // 2 * 2:2]
    margin = jnp.minimum(lengths[giver] - 1, limit - lengths[sink]) // 2
    margin = jnp.where((giver == order[0]) | (sink == order[0]) | (lengths[sink] == 0), 0, jnp.maximum(margin, 0))
    passed = jax.random.randint(jax.random.fold_in(own, 4), (count // 2,), 0, 1 << 20) % (margin + 1)
    lengths = lengths.at[giver].add(-passed).at[sink].add(passed)
    labels = jnp.searchsorted(jnp.cumsum(lengths), jnp.arange(rows * top), side="right").astype(jnp.int32)
    grid = labels.reshape(top, rows).T
    grid = grid[jax.random.permutation(jax.random.fold_in(own, 1), rows)]
    rotation = jax.random.randint(jax.random.fold_in(own, 2), (rows, 1), 0, top)
    return jnp.take_along_axis(grid, (jnp.arange(top)[None, :] + rotation) % top, axis=1)


def load_shares(amount, total, reach, slope, full):
    loads = [(1 << 20) // math.isqrt(rank ** slope) + 1 for rank in range(1, amount + 1)]
    largest = reach if full else min(reach, max(-(-total // amount), total * loads[0] // sum(loads)))
    least = 1 if total - largest >= amount - 1 else 0
    given, surplus = [largest] + [least] * (amount - 1), total - largest - least * (amount - 1)
    while surplus > 0:
        movable = [i for i in range(1, amount) if given[i] < largest] or [i for i in range(1, amount) if given[i] < reach]
        mass, budget = sum([loads[i] for i in movable]), surplus
        for i in movable:
            more = min(reach - given[i], max(1, budget * loads[i] // mass), surplus)
            given[i] = given[i] + more
            surplus = surplus - more
    return np.array(given)


def scatter_about(own_key, extent, scale, limit, cuts=(), held_as=jnp.bfloat16):
    array = scale * jax.random.normal(own_key, extent, jnp.float32)
    if cuts:
        array = array * block_levels(own_key, extent, cuts, -0.22, 0.18)
    return jnp.clip(array, -limit, limit).astype(held_as)


def setup_inputs(seed: int = 0, part: int = 0) -> dict:
    seeds = jax.random.split(jax.random.key(seed), 9)
    own_keys = jax.random.split(jax.random.fold_in(seeds[8], part), 9)
    celerity = jnp.clip(0.1 + 0.35 * jax.random.uniform(seeds[0], (NLON, NLAT), jnp.float32) ** block_levels(seeds[0], (NLON, NLAT), ((0, 16),), -0.2, 0.2), 0.1, 0.45)
    station_tile_keys = jax.random.split(jax.random.fold_in(own_keys[1], 1), OBS_TOTAL // OBS_DEV)
    station_tile_turns = jax.random.permutation(jax.random.fold_in(own_keys[1], 3), OBS_TOTAL // OBS_DEV)
    station_tile = jax.vmap(lambda own, number: deal_out(jax.random.fold_in(own_keys[1], 2), own, number, OBS_DEV, N_LON, 1, CAP, 2))(station_tile_keys, station_tile_turns).reshape((OBS_TOTAL, 1))
    station_block = place_ends(jax.random.randint(own_keys[2], (OBS_TOTAL,), 0, BLK), jax.random.fold_in(own_keys[2], 1), 0, BLK - 1).astype(jnp.int32)
    footprint = jnp.clip(1.0 * jax.random.uniform(own_keys[3], (OBS_TOTAL, 128), jnp.float32) ** block_levels(own_keys[3], (OBS_TOTAL, 128), ((0, 16),), -0.2, 0.2), 0.0, 1.0).astype(jnp.bfloat16)
    misfit = scatter_about(own_keys[4], (STEPS, OBS_TOTAL), 0.2, 1.1953125, ((1, 16),))
    segment_block = place_ends(jax.random.randint(seeds[5], (SEG_TOTAL,), 0, BLK), jax.random.fold_in(seeds[5], 1), 0, BLK - 1).astype(jnp.int32)
    segment_fault = place_ends(jax.random.randint(seeds[6], (SEG_TOTAL,), 0, SUBF), jax.random.fold_in(seeds[6], 1), 0, SUBF - 1).astype(jnp.int32)
    green_uplift = scatter_about(seeds[7], (SEG_TOTAL, 256), 128 ** -0.5, 0.5, ((0, 16),))
    return dict(celerity=celerity, station_tile=station_tile, station_block=station_block, footprint=footprint, misfit=misfit, segment_block=segment_block, segment_fault=segment_fault, green_uplift=green_uplift)


def stencil(previous, current, kappa, force):
    centre = current[1:-1]
    kappa_centre = kappa[1:-1]
    northern = 0.5 * (kappa_centre + kappa[:-2]) * (current[:-2] - centre)
    southern = 0.5 * (kappa_centre + kappa[2:]) * (current[2:] - centre)
    widened = jnp.pad(centre, ((0, 0), (1, 1)))
    kappa_wide = jnp.pad(kappa_centre, ((0, 0), (1, 1)))
    western = 0.5 * (kappa_centre + kappa_wide[:, :-2]) * (widened[:, :-2] - centre)
    eastern = 0.5 * (kappa_centre + kappa_wide[:, 2:]) * (widened[:, 2:] - centre)
    return 2.0 * centre - previous + northern + southern + western + eastern + force


def window_basis(steps, windows):
    row_index = jnp.arange(2 * steps, dtype=jnp.int32)
    col_index = jnp.arange(2 * windows, dtype=jnp.int32)
    rake_row = row_index // steps
    time_row = (row_index % steps).astype(jnp.float32)
    rake_col = col_index // windows
    centre = (col_index % windows).astype(jnp.float32) * (steps - 1) / (windows - 1)
    tent = jnp.maximum(0.0, 1.0 - jnp.abs(time_row[:, None] - centre[None, :]))
    return jnp.where(rake_row[:, None] == rake_col[None, :], tent, 0.0).astype(jnp.float32)


def reference(celerity, station_tile, station_block, footprint, misfit, segment_block, segment_fault, green_uplift):
    nlon_cells = CLON * N_LON
    all_blocks = nlon_cells * NLAT // 128
    target = (station_tile[:, 0] * BLK + station_block).astype(jnp.int32)
    foot = footprint.astype(jnp.float32)

    def one_moment(moment):
        values = misfit[moment].astype(jnp.float32)[:, None] * foot
        return jax.ops.segment_sum(values, target, all_blocks)

    forcing = lax.map(one_moment, jnp.arange(STEPS, dtype=jnp.int32)).reshape(STEPS, nlon_cells, NLAT)
    kappa_pad = jnp.pad(celerity, ((1, 1), (0, 0)))
    previous = jnp.zeros((nlon_cells, NLAT), jnp.float32)
    current = jnp.zeros((nlon_cells, NLAT), jnp.float32)
    record = [None] * STEPS
    for step in range(STEPS):
        moment = STEPS - 1 - step
        padded = jnp.pad(current, ((1, 1), (0, 0)))
        fresh = stencil(previous, padded, kappa_pad, forcing[moment])
        previous, current = current, fresh
        record[moment] = fresh
    history = jnp.stack(record).reshape(STEPS, all_blocks, 128)
    seg_global = (jnp.arange(SEG_TOTAL, dtype=jnp.int32) // SEG_DEV) * BLK + segment_block
    picked = jnp.take(history, seg_global.astype(jnp.int32), axis=1)
    green = green_uplift.astype(jnp.float32).reshape(SEG_TOTAL, 2, 128)
    amps = jnp.einsum("src,tsc->srt", green, picked, precision=lax.Precision.HIGHEST).reshape(SEG_TOTAL, 2 * STEPS)
    terms = jnp.dot(amps, window_basis(STEPS, NWIN), precision=lax.Precision.HIGHEST)
    gradient = jax.ops.segment_sum(terms, segment_fault, SUBF)
    return current, gradient
```

```python
import functools

import jax
import jax.numpy as jnp
from jax import lax
from jax.experimental import pallas as pl
from jax.experimental.pallas import tpu as pltpu
from jax.sharding import PartitionSpec as P

SUB_DEV = 4
NWIN = 32
LANES = 128
RIM = 8
META = 16
HIGH = lax.Precision.HIGHEST


def iota(shape, dim):
    return lax.broadcasted_iota(jnp.int32, shape, dim)


def order(turn, tiles):
    half = tiles // 2
    swing = (turn + 1) // 2
    shift = half + jnp.where(lax.rem(turn, 2) == 1, -swing, swing)
    return jnp.where(turn == tiles - 1, 0, shift)


def kernel(
    tiles,
    cap,
    cel_ref,
    tile_ref,
    block_ref,
    foot_ref,
    mis_ref,
    segb_ref,
    segf_ref,
    green_ref,
    out_ref,
    grad_ref,
    ext,
    placed,
    sent,
    got,
    field,
    rim_out,
    rim_in,
    cel_in,
    past,
    picks,
    part_out,
    part_in,
    send_sem,
    recv_sem,
    rim_send,
    rim_recv,
    cel_send,
    cel_recv,
    part_send,
    part_recv,
):
    me = lax.axis_index("lon")
    rows, lat = cel_ref.shape
    stations = foot_ref.shape[0]
    steps = mis_ref.shape[0]
    segments = green_ref.shape[0]
    chunks = lat // LANES
    wide = rows + 2 * RIM
    pages = -(-cap // LANES)
    page = min(cap, LANES)
    own = slice(RIM, RIM + rows)
    barrier = pltpu.get_barrier_semaphore()

    def partner(shift):
        return lax.rem(me + shift, tiles)

    def greet(shift, carry):
        pl.semaphore_signal(
            barrier,
            inc=1,
            device_id={"lon": partner(shift)},
            device_id_type=pl.DeviceIdType.MESH,
        )
        return carry

    lax.fori_loop(1, tiles, greet, 0)

    span = min(256, stations)
    ramp = (iota((span, span), 0) < iota((span, span), 1)).astype(jnp.bfloat16)
    carry = jnp.zeros((tiles, 1), jnp.float32)
    for start in range(0, stations, span):
        target = tile_ref[:, start : start + span]
        hot = iota((tiles, span), 0) == target
        ones = jnp.where(hot, 1.0, 0.0)
        before = carry + jnp.dot(
            ones.astype(jnp.bfloat16), ramp, preferred_element_type=jnp.float32
        )
        ranked = jnp.sum(jnp.where(hot, before, 0.0), axis=0, keepdims=True)
        placed[:, start : start + span] = target * cap + ranked.astype(jnp.int32)
        carry = carry + jnp.sum(ones, axis=1, keepdims=True)

    blocks = block_ref[...]
    row = lax.div(blocks, chunks).astype(jnp.float32)
    chunk = lax.rem(blocks, chunks).astype(jnp.float32)
    place = iota((8, stations), 0)
    digits = jnp.where(place == 0, row, jnp.where(place == 1, chunk, 0.0))
    meta = jnp.concatenate(
        [
            mis_ref[...].astype(jnp.float32),
            digits,
            jnp.zeros((LANES - steps - 8, stations), jnp.float32),
        ],
        axis=0,
    )
    ext[:, :LANES] = foot_ref[...]
    ext[:, LANES:] = meta.T.astype(jnp.bfloat16)
    field[...] = jnp.zeros_like(field)

    pl.semaphore_wait(barrier, tiles - 1)

    def side_copy(side, source, landing, send, recv):
        return pltpu.make_async_remote_copy(
            src_ref=source,
            dst_ref=landing,
            send_sem=send.at[side],
            recv_sem=recv.at[side],
            device_id={"lon": me - 1 if side == 0 else me + 1},
            device_id_type=pl.DeviceIdType.MESH,
        )

    exists = (me > 0, me < tiles - 1)

    def cel_copy(side):
        rim = slice(0, RIM) if side == 0 else slice(rows - RIM, rows)
        return side_copy(side, cel_ref.at[rim], cel_in.at[side], cel_send, cel_recv)

    def rim_copy(side):
        return side_copy(side, rim_out.at[side], rim_in.at[side], rim_send, rim_recv)

    for side in range(2):

        @pl.when(exists[side])
        def _():
            cel_copy(side).start()

    def obs_copy(turn):
        return pltpu.make_async_remote_copy(
            src_ref=sent.at[turn],
            dst_ref=got.at[turn],
            send_sem=send_sem.at[turn],
            recv_sem=recv_sem.at[turn],
            device_id={"lon": partner(order(turn, tiles))},
            device_id_type=pl.DeviceIdType.MESH,
        )

    def pack(turn, box):
        base = partner(order(turn, tiles)) * cap
        slot_hot = placed[...] == base + iota((cap, stations), 0)
        matrix = jnp.where(slot_hot, 1.0, 0.0).astype(jnp.bfloat16)
        packed = jnp.dot(matrix, ext[...], preferred_element_type=jnp.float32)
        box[turn, :cap, :] = packed[:, :LANES].astype(jnp.bfloat16)
        turned = packed[:, LANES:].T
        for n in range(pages):
            box[turn, cap + n * META : cap + (n + 1) * META, :page] = turned[
                :META, n * page : (n + 1) * page
            ].astype(jnp.bfloat16)

    def pack_and_send(turn, carry):
        pack(turn, sent)
        obs_copy(turn).start()
        return carry

    lax.fori_loop(0, tiles - 1, pack_and_send, 0)
    pack(tiles - 1, got)

    def spread(turn):
        sheets = [
            got[turn, cap + n * META : cap + (n + 1) * META, :][:, :page].astype(jnp.float32)
            for n in range(pages)
        ]
        meta = sheets[0] if pages == 1 else jnp.concatenate(sheets, axis=1)
        key = meta[steps + 1 : steps + 2] * rows + meta[steps : steps + 1]
        hot = key.astype(jnp.int32) == iota((rows * chunks, cap), 0)
        prints = got[turn, :cap, :]
        for moment in range(steps):
            weighted = jnp.where(hot, meta[moment : moment + 1], 0.0).astype(jnp.bfloat16)
            summed = jnp.dot(weighted, prints, preferred_element_type=jnp.float32)
            for c in range(chunks):
                cells = (moment, own, slice(c * LANES, (c + 1) * LANES))
                field[cells] = field[cells] + summed[c * rows : (c + 1) * rows]

    spread(tiles - 1)

    def receive(turn, carry):
        obs_copy(turn).wait_recv()
        spread(turn)
        return carry

    lax.fori_loop(0, tiles - 1, receive, 0)

    last = steps - 1
    level = iota((RIM, lat), 0)
    for n in range(steps // 2):
        t = last - n
        head, tail = field[t, own][:RIM], field[last - t, own][:RIM]
        rim_out[0, n] = jnp.where(level < t, head, pltpu.roll(tail, t, 0))
        head, tail = field[t, own][rows - RIM :], field[last - t, own][rows - RIM :]
        rim_out[1, n] = jnp.where(level >= RIM - t, head, pltpu.roll(tail, RIM - t, 0))
    for side in range(2):

        @pl.when(exists[side])
        def _():
            rim_copy(side).start()

    for side in range(2):

        @pl.when(exists[1 - side])
        def _():
            cel_copy(side).wait_recv()

        @pl.when(jnp.logical_not(exists[1 - side]))
        def _():
            cel_in[side] = jnp.zeros((RIM, lat), jnp.float32)

    kappa = jnp.concatenate([cel_in[1], cel_ref[...], cel_in[0]], axis=0)
    column = iota((wide, lat), 1)
    line = iota((wide, lat), 0) + (me * rows - RIM)
    inside = jnp.logical_and(line >= 0, line < tiles * rows)
    north = 0.5 * (kappa + pltpu.roll(kappa, 1, 0))
    south = 0.5 * (kappa + pltpu.roll(kappa, wide - 1, 0))
    west_edge, east_edge = column == 0, column == lat - 1
    west = 0.5 * (kappa + jnp.where(west_edge, 0.0, pltpu.roll(kappa, 1, 1)))
    east = 0.5 * (kappa + jnp.where(east_edge, 0.0, pltpu.roll(kappa, lat - 1, 1)))
    centre = 2.0 - (north + south + west + east)
    west = jnp.where(west_edge, 0.0, west)
    east = jnp.where(east_edge, 0.0, east)

    for side in range(2):

        @pl.when(exists[1 - side])
        def _():
            rim_copy(side).wait_recv()
            for n in range(steps // 2):
                t = last - n
                tile = rim_in[side, n]
                if side == 0:
                    rim = slice(RIM + rows, wide)
                    field[t, rim] = jnp.where(level < t, tile, 0.0)
                    field[last - t, rim] = jnp.where(
                        level < last - t, pltpu.roll(tile, RIM - t, 0), 0.0
                    )
                else:
                    rim = slice(0, RIM)
                    field[t, rim] = jnp.where(level >= RIM - t, tile, 0.0)
                    field[last - t, rim] = jnp.where(level > t, pltpu.roll(tile, t, 0), 0.0)

    def keep(t, surface):
        for c in range(chunks):
            past[t, c] = surface[own, c * LANES : (c + 1) * LANES]

    keep(last, field[last])

    def advance(step, carry):
        t = last - step
        current = field[t + 1]
        moved = (
            centre * current
            + north * pltpu.roll(current, 1, 0)
            + south * pltpu.roll(current, wide - 1, 0)
            + west * pltpu.roll(current, 1, 1)
            + east * pltpu.roll(current, lat - 1, 1)
            + field[t]
        )
        previous = field[jnp.minimum(t + 2, last)]
        moved = moved - jnp.where(step > 1, previous, 0.0)
        fresh = jnp.where(inside, moved, 0.0)
        field[t] = fresh
        keep(t, fresh)
        return carry

    lax.fori_loop(1, steps, advance, 0)
    out_ref[...] = field[0, own]

    def pick(segment, carry):
        block = segb_ref[segment]
        line, chunk = lax.div(block, chunks), lax.rem(block, chunks)
        for t in range(steps):
            picks[t, pl.ds(segment, 1)] = past[t, chunk, pl.ds(line, 1)]
        return carry

    lax.fori_loop(0, segments, pick, 0)

    lines = tiles * 8
    number = iota((lines, segments), 0)
    fault = jnp.where(
        lax.rem(number, 8) < SUB_DEV, lax.div(number, 8) * SUB_DEV + lax.rem(number, 8), -1
    )
    owner_hot = jnp.where(segf_ref[...] == fault, 1.0, 0.0)
    green = green_ref[...].astype(jnp.float32)
    moment = lax.div(iota((steps * LANES, LANES), 0), LANES).astype(jnp.float32)
    window = iota((steps * LANES, LANES), 1)
    tent_at = lax.rem(window, NWIN).astype(jnp.float32) * (steps - 1) / (NWIN - 1)
    tent = jnp.maximum(0.0, 1.0 - jnp.abs(moment - tent_at))
    total = None
    for rake in range(2):
        weights = green[:, rake * LANES : (rake + 1) * LANES]
        products = jnp.concatenate([picks[t] * weights for t in range(steps)], axis=1)
        by_fault = jnp.dot(owner_hot, products, precision=HIGH, preferred_element_type=jnp.float32)
        basis = jnp.where(lax.div(window, NWIN) == rake, tent, 0.0)
        term = jnp.dot(by_fault, basis, precision=HIGH, preferred_element_type=jnp.float32)
        total = term if total is None else total + term
    part_out[...] = total.reshape(tiles, 8, LANES)

    def part_copy(turn):
        there = partner(order(turn, tiles))
        return pltpu.make_async_remote_copy(
            src_ref=part_out.at[there],
            dst_ref=part_in.at[turn],
            send_sem=part_send.at[turn],
            recv_sem=part_recv.at[turn],
            device_id={"lon": there},
            device_id_type=pl.DeviceIdType.MESH,
        )

    def part_start(turn, carry):
        part_copy(turn).start()
        return carry

    lax.fori_loop(0, tiles - 1, part_start, 0)
    part_in[tiles - 1] = part_out[me]

    def sent_wait(turn, carry):
        obs_copy(turn).wait_send()
        return carry

    lax.fori_loop(0, tiles - 1, sent_wait, 0)
    for side in range(2):

        @pl.when(exists[side])
        def _():
            cel_copy(side).wait_send()
            rim_copy(side).wait_send()

    def part_wait(turn, carry):
        part_copy(turn).wait()
        return carry

    lax.fori_loop(0, tiles - 1, part_wait, 0)
    grad_ref[...] = jnp.sum(part_in[...], axis=0)[:SUB_DEV, : 2 * NWIN]


def local(
    celerity,
    station_tile,
    station_block,
    footprint,
    misfit,
    segment_block,
    segment_fault,
    green_uplift,
):
    tiles = lax.axis_size("lon")
    rows, lat = celerity.shape
    stations = footprint.shape[0]
    steps = misfit.shape[0]
    segments = green_uplift.shape[0]
    cap = 2 * stations // tiles
    depth = cap + META * -(-cap // LANES)
    dma = pltpu.SemaphoreType.DMA
    vmem = pl.BlockSpec(memory_space=pltpu.VMEM)
    return pl.pallas_call(
        functools.partial(kernel, tiles, cap),
        out_shape=(
            jax.ShapeDtypeStruct((rows, lat), jnp.float32),
            jax.ShapeDtypeStruct((SUB_DEV, 2 * NWIN), jnp.float32),
        ),
        in_specs=[vmem] * 5 + [pl.BlockSpec(memory_space=pltpu.SMEM)] + [vmem] * 2,
        out_specs=(vmem, vmem),
        scratch_shapes=[
            pltpu.VMEM((stations, 2 * LANES), jnp.bfloat16),
            pltpu.VMEM((1, stations), jnp.int32),
            pltpu.VMEM((tiles, depth, LANES), jnp.bfloat16),
            pltpu.VMEM((tiles, depth, LANES), jnp.bfloat16),
            pltpu.VMEM((steps, rows + 2 * RIM, lat), jnp.float32),
            pltpu.VMEM((2, steps // 2, RIM, lat), jnp.float32),
            pltpu.VMEM((2, steps // 2, RIM, lat), jnp.float32),
            pltpu.VMEM((2, RIM, lat), jnp.float32),
            pltpu.VMEM((steps, lat // LANES, rows, LANES), jnp.float32),
            pltpu.VMEM((steps, segments, LANES), jnp.float32),
            pltpu.VMEM((tiles, 8, LANES), jnp.float32),
            pltpu.VMEM((tiles, 8, LANES), jnp.float32),
            dma((tiles,)),
            dma((tiles,)),
            dma((2,)),
            dma((2,)),
            dma((2,)),
            dma((2,)),
            dma((tiles,)),
            dma((tiles,)),
        ],
        compiler_params=pltpu.CompilerParams(
            collective_id=0, has_side_effects=True, vmem_limit_bytes=44 * 1024 * 1024
        ),
    )(
        celerity,
        station_tile.reshape(1, stations),
        station_block.reshape(1, stations),
        footprint,
        misfit,
        segment_block,
        segment_fault.reshape(1, segments),
        green_uplift,
    )


def solution(mesh):
    placed = (
        P("lon", None),
        P(("groups", "lon"), None),
        P(("groups", "lon")),
        P(("groups", "lon"), None),
        P(None, ("groups", "lon")),
        P("lon"),
        P("lon"),
        P("lon", None),
    )
    return jax.shard_map(
        local,
        mesh=mesh,
        in_specs=placed,
        out_specs=(P(("groups", "lon"), None), P(("groups", "lon"), None)),
        check_vma=False,
    )
```

```python
import functools

import jax
import jax.numpy as jnp
from jax import lax
from jax.experimental import pallas as pl
from jax.experimental.pallas import tpu as pltpu
from jax.sharding import PartitionSpec as P

SUB_DEV = 4
NWIN = 32
LANES = 128
RIM = 8
META = 16
HIGH = lax.Precision.HIGHEST


def iota(shape, dim):
    return lax.broadcasted_iota(jnp.int32, shape, dim)


def order(turn, tiles):
    half = tiles // 2
    return jnp.where(lax.rem(turn, 2) == 0, half + lax.div(turn, 2), lax.div(turn + 1, 2))


def kernel(
    tiles,
    cap,
    cel_hbm,
    tile_hbm,
    block_hbm,
    foot_hbm,
    mis_hbm,
    segb_hbm,
    segf_hbm,
    green_hbm,
    out_ref,
    grad_ref,
    tile_ref,
    block_ref,
    mis_ref,
    segb_ref,
    segf_ref,
    green_ref,
    kappa_ref,
    coef,
    basis,
    load_sem,
    ext,
    placed,
    sent,
    got,
    field,
    rim_out,
    rim_in,
    past,
    picks,
    part_out,
    part_in,
    send_sem,
    recv_sem,
    rim_send,
    rim_recv,
    cel_send,
    cel_recv,
    part_send,
    part_recv,
):
    me = lax.axis_index("lon")
    rows, lat = cel_hbm.shape
    stations = foot_hbm.shape[0]
    steps = mis_hbm.shape[0]
    segments = green_hbm.shape[0]
    chunks = lat // LANES
    wide = rows + 2 * RIM
    pages = -(-cap // LANES)
    page = min(cap, LANES)
    own = slice(RIM, RIM + rows)
    barrier = pltpu.get_barrier_semaphore()

    loads = [
        pltpu.make_async_copy(source, landing, load_sem.at[n])
        for n, (source, landing) in enumerate(
            (
                (tile_hbm, tile_ref),
                (block_hbm, block_ref),
                (mis_hbm, mis_ref),
                (foot_hbm, ext.at[:, pl.ds(0, LANES)]),
                (cel_hbm, kappa_ref.at[pl.ds(RIM, rows)]),
                (segb_hbm, segb_ref),
                (segf_hbm, segf_ref),
                (green_hbm, green_ref),
            )
        )
    ]
    for load in loads:
        load.start()

    def partner(code):
        there, unit = 0, 1
        while unit < tiles:
            there += lax.rem(lax.div(me, unit) + lax.div(code, unit), 2) * unit
            unit *= 2
        return there

    def greet(shift, carry):
        pl.semaphore_signal(
            barrier,
            inc=1,
            device_id={"lon": partner(shift)},
            device_id_type=pl.DeviceIdType.MESH,
        )
        return carry

    lax.fori_loop(1, tiles, greet, 0)
    for load in loads[:3]:
        load.wait()

    span = min(256, stations)
    ramp = (iota((span, span), 0) < iota((span, span), 1)).astype(jnp.bfloat16)
    carry = jnp.zeros((tiles, 1), jnp.float32)
    for start in range(0, stations, span):
        target = tile_ref[:, start : start + span]
        hot = iota((tiles, span), 0) == target
        ones = jnp.where(hot, 1.0, 0.0)
        before = carry + jnp.dot(
            ones.astype(jnp.bfloat16), ramp, preferred_element_type=jnp.float32
        )
        ranked = jnp.sum(jnp.where(hot, before, 0.0), axis=0, keepdims=True)
        placed[:, start : start + span] = target * cap + ranked.astype(jnp.int32)
        carry = carry + jnp.sum(ones, axis=1, keepdims=True)

    blocks = block_ref[...]
    row = lax.div(blocks, chunks).astype(jnp.float32)
    chunk = lax.rem(blocks, chunks).astype(jnp.float32)
    place = iota((8, stations), 0)
    digits = jnp.where(place == 0, row, jnp.where(place == 1, chunk, 0.0))
    meta = jnp.concatenate(
        [
            mis_ref[...].astype(jnp.float32),
            digits,
            jnp.zeros((LANES - steps - 8, stations), jnp.float32),
        ],
        axis=0,
    )
    ext[:, LANES:] = meta.T.astype(jnp.bfloat16)
    loads[3].wait()

    pl.semaphore_wait(barrier, tiles - 1)

    def side_copy(side, source, landing, send, recv):
        return pltpu.make_async_remote_copy(
            src_ref=source,
            dst_ref=landing,
            send_sem=send.at[side],
            recv_sem=recv.at[side],
            device_id={"lon": me - 1 if side == 0 else me + 1},
            device_id_type=pl.DeviceIdType.MESH,
        )

    exists = (me > 0, me < tiles - 1)

    def cel_copy(side):
        source = cel_hbm.at[pl.ds(0 if side == 0 else rows - RIM, RIM)]
        landing = kappa_ref.at[pl.ds(RIM + rows if side == 0 else 0, RIM)]
        return side_copy(side, source, landing, cel_send.at[0], cel_recv.at[0])

    def rim_copy(side, n):
        return side_copy(
            side, rim_out.at[side, n], rim_in.at[side, n], rim_send.at[n], rim_recv.at[n]
        )

    for side in range(2):

        @pl.when(exists[side])
        def _():
            cel_copy(side).start()

    def obs_copy(code):
        return pltpu.make_async_remote_copy(
            src_ref=sent.at[code],
            dst_ref=got.at[code],
            send_sem=send_sem.at[code],
            recv_sem=recv_sem.at[code],
            device_id={"lon": partner(code)},
            device_id_type=pl.DeviceIdType.MESH,
        )

    def pack(code, there, box):
        slot_hot = placed[...] == there * cap + iota((cap, stations), 0)
        matrix = jnp.where(slot_hot, 1.0, 0.0).astype(jnp.bfloat16)
        packed = jnp.dot(matrix, ext[...], preferred_element_type=jnp.float32)
        box[code, :cap, :] = packed[:, :LANES].astype(jnp.bfloat16)
        turned = packed[:, LANES:].T
        for n in range(pages):
            box[code, cap + n * META : cap + (n + 1) * META, :page] = turned[
                :META, n * page : (n + 1) * page
            ].astype(jnp.bfloat16)

    def pack_and_send(turn, carry):
        code = order(turn, tiles)
        pack(code, partner(code), sent)
        obs_copy(code).start()
        return carry

    lax.fori_loop(0, tiles - 1, pack_and_send, 0)
    pack(0, me, got)

    def weigh(code):
        sheets = [
            got[code, cap + n * META : cap + (n + 1) * META, :][:, :page].astype(jnp.float32)
            for n in range(pages)
        ]
        meta = sheets[0] if pages == 1 else jnp.concatenate(sheets, axis=1)
        key = meta[steps + 1 : steps + 2] * rows + meta[steps : steps + 1]
        return key.astype(jnp.int32) == iota((rows * chunks, cap), 0), meta

    def spread(code, first):
        near, far = weigh(code), weigh(code + 1)
        for moment in range(steps):
            summed = None
            for n, (hot, meta) in enumerate((near, far)):
                weighted = jnp.where(hot, meta[moment : moment + 1], 0.0).astype(jnp.bfloat16)
                term = jnp.dot(
                    weighted, got[code + n, :cap, :], preferred_element_type=jnp.float32
                )
                summed = term if summed is None else summed + term
            for c in range(chunks):
                cells = (moment, own, slice(c * LANES, (c + 1) * LANES))
                piece = summed[c * rows : (c + 1) * rows]
                field[cells] = piece if first else field[cells] + piece

    for load in loads[4:]:
        load.wait()
    for side in range(2):
        rim = slice(RIM + rows, wide) if side == 0 else slice(0, RIM)

        @pl.when(exists[1 - side])
        def _():
            cel_copy(side).wait_recv()

        @pl.when(jnp.logical_not(exists[1 - side]))
        def _():
            kappa_ref[rim] = jnp.zeros((RIM, lat), jnp.float32)
            field[:, rim] = jnp.zeros((steps, RIM, lat), jnp.float32)

    kappa = kappa_ref[...]
    column = iota((wide, lat), 1)
    north = 0.5 * (kappa + pltpu.roll(kappa, 1, 0))
    south = 0.5 * (kappa + pltpu.roll(kappa, wide - 1, 0))
    west_edge, east_edge = column == 0, column == lat - 1
    west = 0.5 * (kappa + jnp.where(west_edge, 0.0, pltpu.roll(kappa, 1, 1)))
    east = 0.5 * (kappa + jnp.where(east_edge, 0.0, pltpu.roll(kappa, lat - 1, 1)))
    coef[0] = 2.0 - (north + south + west + east)
    coef[1] = north
    coef[2] = south
    coef[3] = jnp.where(west_edge, 0.0, west)
    coef[4] = jnp.where(east_edge, 0.0, east)

    moment = lax.div(iota((steps * LANES, LANES), 0), LANES).astype(jnp.float32)
    window = iota((steps * LANES, LANES), 1)
    tent_at = lax.rem(window, NWIN).astype(jnp.float32) * (steps - 1) / (NWIN - 1)
    tent = jnp.maximum(0.0, 1.0 - jnp.abs(moment - tent_at))
    for rake in range(2):
        basis[rake] = jnp.where(lax.div(window, NWIN) == rake, tent, 0.0)

    obs_copy(1).wait_recv()
    spread(0, True)

    def receive(pair, carry):
        obs_copy(2 * pair).wait_recv()
        obs_copy(2 * pair + 1).wait_recv()
        spread(2 * pair, False)
        return carry

    lax.fori_loop(1, tiles // 2, receive, 0)

    last = steps - 1
    level = iota((RIM, lat), 0)
    for n in range(steps // 2):
        t = last - n
        head, tail = field[t, own][:RIM], field[last - t, own][:RIM]
        rim_out[0, n] = jnp.where(level < t, head, pltpu.roll(tail, t, 0))
        head, tail = field[t, own][rows - RIM :], field[last - t, own][rows - RIM :]
        rim_out[1, n] = jnp.where(level >= RIM - t, head, pltpu.roll(tail, RIM - t, 0))
        for side in range(2):

            @pl.when(exists[side])
            def _():
                rim_copy(side, n).start()

    def land(n):
        t = last - n
        for side in range(2):

            @pl.when(exists[1 - side])
            def _():
                rim_copy(side, n).wait_recv()
                tile = rim_in[side, n]
                if side == 0:
                    rim = slice(RIM + rows, wide)
                    field[t, rim] = jnp.where(level < t, tile, 0.0)
                    field[last - t, rim] = jnp.where(
                        level < last - t, pltpu.roll(tile, RIM - t, 0), 0.0
                    )
                else:
                    rim = slice(0, RIM)
                    field[t, rim] = jnp.where(level >= RIM - t, tile, 0.0)
                    field[last - t, rim] = jnp.where(level > t, pltpu.roll(tile, t, 0), 0.0)

    line = iota((wide, lat), 0) + (me * rows - RIM)
    inside = jnp.logical_and(line >= 0, line < tiles * rows)

    def keep(t, surface):
        for c in range(chunks):
            past[t, c] = surface[own, c * LANES : (c + 1) * LANES]

    def advance(step, carry):
        t = last - step
        current = field[t + 1]
        moved = (
            coef[0] * current
            + coef[1] * pltpu.roll(current, 1, 0)
            + coef[2] * pltpu.roll(current, wide - 1, 0)
            + coef[3] * pltpu.roll(current, 1, 1)
            + coef[4] * pltpu.roll(current, lat - 1, 1)
            + field[t]
        )
        if not isinstance(step, int) or step > 1:
            moved = moved - field[t + 2]
        fresh = jnp.where(inside, moved, 0.0)
        field[t] = fresh
        keep(t, fresh)
        return carry

    land(0)
    keep(last, field[last])
    for n in range(1, steps // 2):
        land(n)
        advance(n, 0)
    lax.fori_loop(steps // 2, steps, advance, 0)
    out_ref[...] = field[0, own]

    def pick(segment, carry):
        block = segb_ref[segment]
        line, chunk = lax.div(block, chunks), lax.rem(block, chunks)
        for t in range(steps):
            picks[t, pl.ds(segment, 1)] = past[t, chunk, pl.ds(line, 1)]
        return carry

    lax.fori_loop(0, segments, pick, 0)

    lines = tiles * 8
    number = iota((lines, segments), 0)
    fault = jnp.where(
        lax.rem(number, 8) < SUB_DEV, lax.div(number, 8) * SUB_DEV + lax.rem(number, 8), -1
    )
    owner_hot = jnp.where(segf_ref[...] == fault, 1.0, 0.0)
    green = green_ref[...].astype(jnp.float32)
    total = None
    for rake in range(2):
        weights = green[:, rake * LANES : (rake + 1) * LANES]
        products = jnp.concatenate([picks[t] * weights for t in range(steps)], axis=1)
        by_fault = jnp.dot(owner_hot, products, precision=HIGH, preferred_element_type=jnp.float32)
        term = jnp.dot(by_fault, basis[rake], precision=HIGH, preferred_element_type=jnp.float32)
        total = term if total is None else total + term
    part_out[...] = total.reshape(tiles, 8, LANES)

    def part_copy(code):
        there = partner(code)
        return pltpu.make_async_remote_copy(
            src_ref=part_out.at[there],
            dst_ref=part_in.at[code],
            send_sem=part_send.at[code],
            recv_sem=part_recv.at[code],
            device_id={"lon": there},
            device_id_type=pl.DeviceIdType.MESH,
        )

    def part_start(turn, carry):
        part_copy(order(turn, tiles)).start()
        return carry

    lax.fori_loop(0, tiles - 1, part_start, 0)
    part_in[0] = part_out[me]

    def sent_wait(code, carry):
        obs_copy(code).wait_send()
        return carry

    lax.fori_loop(1, tiles, sent_wait, 0)
    for side in range(2):

        @pl.when(exists[side])
        def _():
            cel_copy(side).wait_send()
            for n in range(steps // 2):
                rim_copy(side, n).wait_send()

    def part_wait(code, carry):
        part_copy(code).wait()
        return carry

    lax.fori_loop(1, tiles, part_wait, 0)
    grad_ref[...] = jnp.sum(part_in[...], axis=0)[:SUB_DEV, : 2 * NWIN]


def local(
    celerity,
    station_tile,
    station_block,
    footprint,
    misfit,
    segment_block,
    segment_fault,
    green_uplift,
):
    tiles = lax.axis_size("lon")
    rows, lat = celerity.shape
    stations = footprint.shape[0]
    steps = misfit.shape[0]
    segments = green_uplift.shape[0]
    cap = 2 * stations // tiles
    depth = cap + META * -(-cap // LANES)
    dma = pltpu.SemaphoreType.DMA
    vmem = pl.BlockSpec(memory_space=pltpu.VMEM)
    return pl.pallas_call(
        functools.partial(kernel, tiles, cap),
        out_shape=(
            jax.ShapeDtypeStruct((rows, lat), jnp.float32),
            jax.ShapeDtypeStruct((SUB_DEV, 2 * NWIN), jnp.float32),
        ),
        in_specs=[pl.BlockSpec(memory_space=pltpu.HBM)] * 8,
        out_specs=(vmem, vmem),
        scratch_shapes=[
            pltpu.VMEM((1, stations), jnp.int32),
            pltpu.VMEM((1, stations), jnp.int32),
            pltpu.VMEM((steps, stations), jnp.bfloat16),
            pltpu.SMEM((segments,), jnp.int32),
            pltpu.VMEM((1, segments), jnp.int32),
            pltpu.VMEM((segments, 2 * LANES), jnp.bfloat16),
            pltpu.VMEM((rows + 2 * RIM, lat), jnp.float32),
            pltpu.VMEM((5, rows + 2 * RIM, lat), jnp.float32),
            pltpu.VMEM((2, steps * LANES, LANES), jnp.float32),
            dma((8,)),
            pltpu.VMEM((stations, 2 * LANES), jnp.bfloat16),
            pltpu.VMEM((1, stations), jnp.int32),
            pltpu.VMEM((tiles, depth, LANES), jnp.bfloat16),
            pltpu.VMEM((tiles, depth, LANES), jnp.bfloat16),
            pltpu.VMEM((steps, rows + 2 * RIM, lat), jnp.float32),
            pltpu.VMEM((2, steps // 2, RIM, lat), jnp.float32),
            pltpu.VMEM((2, steps // 2, RIM, lat), jnp.float32),
            pltpu.VMEM((steps, lat // LANES, rows, LANES), jnp.float32),
            pltpu.VMEM((steps, segments, LANES), jnp.float32),
            pltpu.VMEM((tiles, 8, LANES), jnp.float32),
            pltpu.VMEM((tiles, 8, LANES), jnp.float32),
            dma((tiles,)),
            dma((tiles,)),
            dma((steps // 2, 2)),
            dma((steps // 2, 2)),
            dma((1, 2)),
            dma((1, 2)),
            dma((tiles,)),
            dma((tiles,)),
        ],
        compiler_params=pltpu.CompilerParams(
            collective_id=0, has_side_effects=True, vmem_limit_bytes=44 * 1024 * 1024
        ),
    )(
        celerity,
        station_tile.reshape(1, stations),
        station_block.reshape(1, stations),
        footprint,
        misfit,
        segment_block,
        segment_fault.reshape(1, segments),
        green_uplift,
    )


def solution(mesh):
    placed = (
        P("lon", None),
        P(("groups", "lon"), None),
        P(("groups", "lon")),
        P(("groups", "lon"), None),
        P(None, ("groups", "lon")),
        P("lon"),
        P("lon"),
        P("lon", None),
    )
    return jax.shard_map(
        local,
        mesh=mesh,
        in_specs=placed,
        out_specs=(P(("groups", "lon"), None), P(("groups", "lon"), None)),
        check_vma=False,
    )
```

```python
import functools

import jax
import jax.numpy as jnp
from jax import lax
from jax.experimental import pallas as pl
from jax.experimental.pallas import tpu as pltpu
from jax.sharding import PartitionSpec as P

SUB_DEV = 4
NWIN = 32
LANES = 128
RIM = 8
META = 16
HIGH = lax.Precision.HIGHEST


def iota(shape, dim):
    return lax.broadcasted_iota(jnp.int32, shape, dim)


def order(turn, tiles):
    half = tiles // 2
    return jnp.where(lax.rem(turn, 2) == 0, half + lax.div(turn, 2), lax.div(turn + 1, 2))


def kernel(
    tiles,
    cap,
    cel_hbm,
    tile_hbm,
    block_hbm,
    foot_hbm,
    mis_hbm,
    segb_hbm,
    segf_hbm,
    green_hbm,
    out_ref,
    grad_ref,
    tile_ref,
    block_ref,
    mis_ref,
    segb_ref,
    segf_ref,
    green_ref,
    kappa_ref,
    coef,
    basis,
    load_sem,
    ext,
    placed,
    sent,
    got,
    field,
    rim_out,
    rim_in,
    past,
    picks,
    part_out,
    part_in,
    send_sem,
    recv_sem,
    rim_send,
    rim_recv,
    cel_send,
    cel_recv,
    part_send,
    part_recv,
):
    me = lax.axis_index("lon")
    rows, lat = cel_hbm.shape
    stations = foot_hbm.shape[0]
    steps = mis_hbm.shape[0]
    segments = green_hbm.shape[0]
    chunks = lat // LANES
    wide = rows + 2 * RIM
    pages = -(-cap // LANES)
    page = min(cap, LANES)
    own = slice(RIM, RIM + rows)
    barrier = pltpu.get_barrier_semaphore()

    loads = [
        pltpu.make_async_copy(source, landing, load_sem.at[n])
        for n, (source, landing) in enumerate(
            (
                (tile_hbm, tile_ref),
                (block_hbm, block_ref),
                (mis_hbm, mis_ref),
                (foot_hbm, ext.at[:, pl.ds(0, LANES)]),
                (cel_hbm, kappa_ref.at[pl.ds(RIM, rows)]),
                (segb_hbm, segb_ref),
                (segf_hbm, segf_ref),
                (green_hbm, green_ref),
            )
        )
    ]
    for load in loads:
        load.start()

    units = [1 << n for n in range(tiles.bit_length() - 1)]
    bits = [lax.rem(lax.div(me, unit), 2) for unit in units]

    def partner(code):
        there = me
        for unit, bit in zip(units, bits):
            if isinstance(code, int):
                there = there + (unit - 2 * unit * bit if code & unit else 0)
            else:
                there = there + lax.rem(lax.div(code, unit), 2) * (unit - 2 * unit * bit)
        return there

    def others(work):
        if tiles <= 16:
            for turn in range(tiles - 1):
                work(tiles // 2 + turn // 2 if turn % 2 == 0 else turn // 2 + 1)
        else:
            lax.fori_loop(1, tiles, lambda code, carry: (work(code), carry)[1], 0)

    def greet(code):
        pl.semaphore_signal(
            barrier,
            inc=1,
            device_id={"lon": partner(code)},
            device_id_type=pl.DeviceIdType.MESH,
        )

    others(greet)
    for load in loads[:3]:
        load.wait()

    span = min(256, stations)
    ramp = (iota((span, span), 0) < iota((span, span), 1)).astype(jnp.bfloat16)
    carry = jnp.zeros((tiles, 1), jnp.float32)
    for start in range(0, stations, span):
        target = tile_ref[:, start : start + span]
        hot = iota((tiles, span), 0) == target
        ones = jnp.where(hot, 1.0, 0.0)
        before = carry + jnp.dot(
            ones.astype(jnp.bfloat16), ramp, preferred_element_type=jnp.float32
        )
        ranked = jnp.sum(jnp.where(hot, before, 0.0), axis=0, keepdims=True)
        placed[:, start : start + span] = target * cap + ranked.astype(jnp.int32)
        carry = carry + jnp.sum(ones, axis=1, keepdims=True)

    blocks = block_ref[...]
    row = lax.div(blocks, chunks).astype(jnp.float32)
    chunk = lax.rem(blocks, chunks).astype(jnp.float32)
    place = iota((8, stations), 0)
    digits = jnp.where(place == 0, row, jnp.where(place == 1, chunk, 0.0))
    meta = jnp.concatenate(
        [
            mis_ref[...].astype(jnp.float32),
            digits,
            jnp.zeros((LANES - steps - 8, stations), jnp.float32),
        ],
        axis=0,
    )
    ext[:, LANES:] = meta.T.astype(jnp.bfloat16)
    loads[3].wait()

    def side_copy(side, source, landing, send, recv):
        return pltpu.make_async_remote_copy(
            src_ref=source,
            dst_ref=landing,
            send_sem=send.at[side],
            recv_sem=recv.at[side],
            device_id={"lon": me - 1 if side == 0 else me + 1},
            device_id_type=pl.DeviceIdType.MESH,
        )

    exists = (me > 0, me < tiles - 1)

    def cel_copy(side):
        source = cel_hbm.at[pl.ds(0 if side == 0 else rows - RIM, RIM)]
        landing = kappa_ref.at[pl.ds(RIM + rows if side == 0 else 0, RIM)]
        return side_copy(side, source, landing, cel_send.at[0], cel_recv.at[0])

    def rim_copy(side, n):
        return side_copy(
            side, rim_out.at[side, n], rim_in.at[side, n], rim_send.at[n], rim_recv.at[n]
        )

    def obs_copy(code):
        return pltpu.make_async_remote_copy(
            src_ref=sent.at[code],
            dst_ref=got.at[code],
            send_sem=send_sem.at[code],
            recv_sem=recv_sem.at[code],
            device_id={"lon": partner(code)},
            device_id_type=pl.DeviceIdType.MESH,
        )

    def pack(code, there, box):
        slot_hot = placed[...] == there * cap + iota((cap, stations), 0)
        matrix = jnp.where(slot_hot, 1.0, 0.0).astype(jnp.bfloat16)
        packed = jnp.dot(matrix, ext[...], preferred_element_type=jnp.float32)
        box[code, :cap, :] = packed[:, :LANES].astype(jnp.bfloat16)
        turned = packed[:, LANES:].T
        for n in range(pages):
            box[code, cap + n * META : cap + (n + 1) * META, :page] = turned[
                :META, n * page : (n + 1) * page
            ].astype(jnp.bfloat16)

    def pack_and_send(turn, carry):
        code = order(turn, tiles)
        pack(code, partner(code), sent)
        obs_copy(code).start()
        return carry

    pack(tiles // 2, partner(tiles // 2), sent)
    pl.semaphore_wait(barrier, tiles - 1)
    for side in range(2):

        @pl.when(exists[side])
        def _():
            cel_copy(side).start()

    obs_copy(tiles // 2).start()
    lax.fori_loop(1, tiles - 1, pack_and_send, 0)
    pack(0, me, got)

    def weigh(code):
        sheets = [
            got[code, cap + n * META : cap + (n + 1) * META, :][:, :page].astype(jnp.float32)
            for n in range(pages)
        ]
        meta = sheets[0] if pages == 1 else jnp.concatenate(sheets, axis=1)
        key = meta[steps + 1 : steps + 2] * rows + meta[steps : steps + 1]
        return key.astype(jnp.int32) == iota((rows * chunks, cap), 0), meta

    def spread(code, first):
        near, far = weigh(code), weigh(code + 1)
        for moment in range(steps):
            summed = None
            for n, (hot, meta) in enumerate((near, far)):
                weighted = jnp.where(hot, meta[moment : moment + 1], 0.0).astype(jnp.bfloat16)
                term = jnp.dot(
                    weighted, got[code + n, :cap, :], preferred_element_type=jnp.float32
                )
                summed = term if summed is None else summed + term
            for c in range(chunks):
                cells = (moment, own, slice(c * LANES, (c + 1) * LANES))
                piece = summed[c * rows : (c + 1) * rows]
                field[cells] = piece if first else field[cells] + piece

    for load in loads[4:]:
        load.wait()
    for side in range(2):
        rim = slice(RIM + rows, wide) if side == 0 else slice(0, RIM)

        @pl.when(exists[1 - side])
        def _():
            cel_copy(side).wait_recv()

        @pl.when(jnp.logical_not(exists[1 - side]))
        def _():
            kappa_ref[rim] = jnp.zeros((RIM, lat), jnp.float32)
            field[:, rim] = jnp.zeros((steps, RIM, lat), jnp.float32)

    kappa = kappa_ref[...]
    column = iota((wide, lat), 1)
    north = 0.5 * (kappa + pltpu.roll(kappa, 1, 0))
    south = 0.5 * (kappa + pltpu.roll(kappa, wide - 1, 0))
    west_edge, east_edge = column == 0, column == lat - 1
    west = 0.5 * (kappa + jnp.where(west_edge, 0.0, pltpu.roll(kappa, 1, 1)))
    east = 0.5 * (kappa + jnp.where(east_edge, 0.0, pltpu.roll(kappa, lat - 1, 1)))
    coef[0] = 2.0 - (north + south + west + east)
    coef[1] = north
    coef[2] = south
    coef[3] = jnp.where(west_edge, 0.0, west)
    coef[4] = jnp.where(east_edge, 0.0, east)

    moment = lax.div(iota((steps * LANES, LANES), 0), LANES).astype(jnp.float32)
    window = iota((steps * LANES, LANES), 1)
    tent_at = lax.rem(window, NWIN).astype(jnp.float32) * (steps - 1) / (NWIN - 1)
    tent = jnp.maximum(0.0, 1.0 - jnp.abs(moment - tent_at))
    for rake in range(2):
        basis[rake] = jnp.where(lax.div(window, NWIN) == rake, tent, 0.0)

    obs_copy(1).wait_recv()
    spread(0, True)

    def receive(pair, carry):
        obs_copy(2 * pair).wait_recv()
        obs_copy(2 * pair + 1).wait_recv()
        spread(2 * pair, False)
        return carry

    lax.fori_loop(1, tiles // 2, receive, 0)

    last = steps - 1
    level = iota((RIM, lat), 0)
    for n in range(steps // 2):
        t = last - n
        head, tail = field[t, own][:RIM], field[last - t, own][:RIM]
        rim_out[0, n] = jnp.where(level < t, head, pltpu.roll(tail, t, 0))
        head, tail = field[t, own][rows - RIM :], field[last - t, own][rows - RIM :]
        rim_out[1, n] = jnp.where(level >= RIM - t, head, pltpu.roll(tail, RIM - t, 0))
        for side in range(2):

            @pl.when(exists[side])
            def _():
                rim_copy(side, n).start()

    def land(n):
        t = last - n
        for side in range(2):

            @pl.when(exists[1 - side])
            def _():
                rim_copy(side, n).wait_recv()
                tile = rim_in[side, n]
                if side == 0:
                    rim = slice(RIM + rows, wide)
                    field[t, rim] = jnp.where(level < t, tile, 0.0)
                    field[last - t, rim] = jnp.where(
                        level < last - t, pltpu.roll(tile, RIM - t, 0), 0.0
                    )
                else:
                    rim = slice(0, RIM)
                    field[t, rim] = jnp.where(level >= RIM - t, tile, 0.0)
                    field[last - t, rim] = jnp.where(level > t, pltpu.roll(tile, t, 0), 0.0)

    line = iota((wide, lat), 0) + (me * rows - RIM)
    inside = jnp.logical_and(line >= 0, line < tiles * rows)

    def keep(t, surface):
        for c in range(chunks):
            past[t, c] = surface[own, c * LANES : (c + 1) * LANES]

    def advance(step, carry):
        t = last - step
        current = field[t + 1]
        moved = (
            coef[0] * current
            + coef[1] * pltpu.roll(current, 1, 0)
            + coef[2] * pltpu.roll(current, wide - 1, 0)
            + coef[3] * pltpu.roll(current, 1, 1)
            + coef[4] * pltpu.roll(current, lat - 1, 1)
            + field[t]
        )
        if not isinstance(step, int) or step > 1:
            moved = moved - field[t + 2]
        fresh = jnp.where(inside, moved, 0.0)
        field[t] = fresh
        keep(t, fresh)
        return carry

    land(0)
    keep(last, field[last])
    for n in range(1, steps // 2):
        land(n)
        advance(n, 0)
    lax.fori_loop(steps // 2, steps, advance, 0)
    out_ref[...] = field[0, own]

    def pick(segment, carry):
        block = segb_ref[segment]
        line, chunk = lax.div(block, chunks), lax.rem(block, chunks)
        for t in range(steps):
            picks[t, pl.ds(segment, 1)] = past[t, chunk, pl.ds(line, 1)]
        return carry

    lax.fori_loop(0, segments, pick, 0)

    lines = tiles * 8
    number = iota((lines, segments), 0)
    fault = jnp.where(
        lax.rem(number, 8) < SUB_DEV, lax.div(number, 8) * SUB_DEV + lax.rem(number, 8), -1
    )
    owner_hot = jnp.where(segf_ref[...] == fault, 1.0, 0.0)
    green = green_ref[...].astype(jnp.float32)
    total = None
    for rake in range(2):
        weights = green[:, rake * LANES : (rake + 1) * LANES]
        products = jnp.concatenate([picks[t] * weights for t in range(steps)], axis=1)
        by_fault = jnp.dot(owner_hot, products, precision=HIGH, preferred_element_type=jnp.float32)
        term = jnp.dot(by_fault, basis[rake], precision=HIGH, preferred_element_type=jnp.float32)
        total = term if total is None else total + term
    part_out[...] = total.reshape(tiles, 8, LANES)

    def part_copy(code):
        there = partner(code)
        return pltpu.make_async_remote_copy(
            src_ref=part_out.at[there],
            dst_ref=part_in.at[code],
            send_sem=part_send.at[code],
            recv_sem=part_recv.at[code],
            device_id={"lon": there},
            device_id_type=pl.DeviceIdType.MESH,
        )

    others(lambda code: part_copy(code).start())
    part_in[0] = part_out[me]

    others(lambda code: obs_copy(code).wait_send())
    for side in range(2):

        @pl.when(exists[side])
        def _():
            cel_copy(side).wait_send()
            for n in range(steps // 2):
                rim_copy(side, n).wait_send()

    others(lambda code: part_copy(code).wait())
    grad_ref[...] = jnp.sum(part_in[...], axis=0)[:SUB_DEV, : 2 * NWIN]


def local(
    celerity,
    station_tile,
    station_block,
    footprint,
    misfit,
    segment_block,
    segment_fault,
    green_uplift,
):
    tiles = lax.axis_size("lon")
    rows, lat = celerity.shape
    stations = footprint.shape[0]
    steps = misfit.shape[0]
    segments = green_uplift.shape[0]
    cap = 2 * stations // tiles
    depth = cap + META * -(-cap // LANES)
    dma = pltpu.SemaphoreType.DMA
    vmem = pl.BlockSpec(memory_space=pltpu.VMEM)
    return pl.pallas_call(
        functools.partial(kernel, tiles, cap),
        out_shape=(
            jax.ShapeDtypeStruct((rows, lat), jnp.float32),
            jax.ShapeDtypeStruct((SUB_DEV, 2 * NWIN), jnp.float32),
        ),
        in_specs=[pl.BlockSpec(memory_space=pltpu.HBM)] * 8,
        out_specs=(vmem, vmem),
        scratch_shapes=[
            pltpu.VMEM((1, stations), jnp.int32),
            pltpu.VMEM((1, stations), jnp.int32),
            pltpu.VMEM((steps, stations), jnp.bfloat16),
            pltpu.SMEM((segments,), jnp.int32),
            pltpu.VMEM((1, segments), jnp.int32),
            pltpu.VMEM((segments, 2 * LANES), jnp.bfloat16),
            pltpu.VMEM((rows + 2 * RIM, lat), jnp.float32),
            pltpu.VMEM((5, rows + 2 * RIM, lat), jnp.float32),
            pltpu.VMEM((2, steps * LANES, LANES), jnp.float32),
            dma((8,)),
            pltpu.VMEM((stations, 2 * LANES), jnp.bfloat16),
            pltpu.VMEM((1, stations), jnp.int32),
            pltpu.VMEM((tiles, depth, LANES), jnp.bfloat16),
            pltpu.VMEM((tiles, depth, LANES), jnp.bfloat16),
            pltpu.VMEM((steps, rows + 2 * RIM, lat), jnp.float32),
            pltpu.VMEM((2, steps // 2, RIM, lat), jnp.float32),
            pltpu.VMEM((2, steps // 2, RIM, lat), jnp.float32),
            pltpu.VMEM((steps, lat // LANES, rows, LANES), jnp.float32),
            pltpu.VMEM((steps, segments, LANES), jnp.float32),
            pltpu.VMEM((tiles, 8, LANES), jnp.float32),
            pltpu.VMEM((tiles, 8, LANES), jnp.float32),
            dma((tiles,)),
            dma((tiles,)),
            dma((steps // 2, 2)),
            dma((steps // 2, 2)),
            dma((1, 2)),
            dma((1, 2)),
            dma((tiles,)),
            dma((tiles,)),
        ],
        compiler_params=pltpu.CompilerParams(
            collective_id=0, has_side_effects=True, vmem_limit_bytes=64 * 1024 * 1024
        ),
    )(
        celerity,
        station_tile.reshape(1, stations),
        station_block.reshape(1, stations),
        footprint,
        misfit,
        segment_block,
        segment_fault.reshape(1, segments),
        green_uplift,
    )


def solution(mesh):
    placed = (
        P("lon", None),
        P(("groups", "lon"), None),
        P(("groups", "lon")),
        P(("groups", "lon"), None),
        P(None, ("groups", "lon")),
        P("lon"),
        P("lon"),
        P("lon", None),
    )
    return jax.shard_map(
        local,
        mesh=mesh,
        in_specs=placed,
        out_specs=(P(("groups", "lon"), None), P(("groups", "lon"), None)),
        check_vma=False,
    )
```

```python
import functools

import jax
import jax.numpy as jnp
from jax import lax
from jax.experimental import pallas as pl
from jax.experimental.pallas import tpu as pltpu
from jax.sharding import PartitionSpec as P

SUB_DEV = 4
NWIN = 32
LANES = 128
RIM = 8
META = 16
HIGH = lax.Precision.HIGHEST


def iota(shape, dim):
    return lax.broadcasted_iota(jnp.int32, shape, dim)


def order(turn, tiles):
    half = tiles // 2
    return jnp.where(lax.rem(turn, 2) == 0, half + lax.div(turn, 2), lax.div(turn + 1, 2))


def kernel(
    tiles,
    cap,
    cel_hbm,
    tile_hbm,
    block_hbm,
    foot_hbm,
    mis_hbm,
    segb_hbm,
    segf_hbm,
    green_hbm,
    out_ref,
    grad_ref,
    tile_ref,
    block_ref,
    mis_ref,
    segb_ref,
    segf_ref,
    green_ref,
    kappa_ref,
    coef,
    basis,
    load_sem,
    ext,
    placed,
    sent,
    got,
    field,
    rim_out,
    rim_in,
    past,
    picks,
    part_out,
    part_in,
    send_sem,
    recv_sem,
    rim_send,
    rim_recv,
    cel_send,
    cel_recv,
    part_send,
    part_recv,
):
    me = lax.axis_index("lon")
    rows, lat = cel_hbm.shape
    stations = foot_hbm.shape[0]
    steps = mis_hbm.shape[0]
    segments = green_hbm.shape[0]
    chunks = lat // LANES
    wide = rows + 2 * RIM
    pages = -(-cap // LANES)
    page = min(cap, LANES)
    own = slice(RIM, RIM + rows)
    barrier = pltpu.get_barrier_semaphore()

    loads = [
        pltpu.make_async_copy(source, landing, load_sem.at[n])
        for n, (source, landing) in enumerate(
            (
                (tile_hbm, tile_ref),
                (block_hbm, block_ref),
                (mis_hbm, mis_ref),
                (foot_hbm, ext.at[:, pl.ds(0, LANES)]),
                (cel_hbm, kappa_ref.at[pl.ds(RIM, rows)]),
                (segb_hbm, segb_ref),
                (segf_hbm, segf_ref),
                (green_hbm, green_ref),
            )
        )
    ]
    for load in loads:
        load.start()

    units = [1 << n for n in range(tiles.bit_length() - 1)]
    bits = [lax.rem(lax.div(me, unit), 2) for unit in units]

    def partner(code):
        there = me
        for unit, bit in zip(units, bits):
            if isinstance(code, int):
                there = there + (unit - 2 * unit * bit if code & unit else 0)
            else:
                there = there + lax.rem(lax.div(code, unit), 2) * (unit - 2 * unit * bit)
        return there

    def others(work):
        if tiles <= 16:
            for turn in range(tiles - 1):
                work(tiles // 2 + turn // 2 if turn % 2 == 0 else turn // 2 + 1)
        else:
            lax.fori_loop(1, tiles, lambda code, carry: (work(code), carry)[1], 0)

    def greet(code):
        pl.semaphore_signal(
            barrier,
            inc=1,
            device_id={"lon": partner(code)},
            device_id_type=pl.DeviceIdType.MESH,
        )

    others(greet)
    for load in loads[:3]:
        load.wait()

    span = min(256, stations)
    ramp = (iota((span, span), 0) < iota((span, span), 1)).astype(jnp.bfloat16)
    carry = jnp.zeros((tiles, 1), jnp.float32)
    for start in range(0, stations, span):
        target = tile_ref[:, start : start + span]
        hot = iota((tiles, span), 0) == target
        ones = jnp.where(hot, 1.0, 0.0)
        before = carry + jnp.dot(
            ones.astype(jnp.bfloat16), ramp, preferred_element_type=jnp.float32
        )
        ranked = jnp.sum(jnp.where(hot, before, 0.0), axis=0, keepdims=True)
        placed[:, start : start + span] = target * cap + ranked.astype(jnp.int32)
        carry = carry + jnp.sum(ones, axis=1, keepdims=True)

    blocks = block_ref[...]
    row = lax.div(blocks, chunks).astype(jnp.float32)
    chunk = lax.rem(blocks, chunks).astype(jnp.float32)
    place = iota((8, stations), 0)
    digits = jnp.where(place == 0, row, jnp.where(place == 1, chunk, 0.0))
    meta = jnp.concatenate(
        [
            mis_ref[...].astype(jnp.float32),
            digits,
            jnp.zeros((LANES - steps - 8, stations), jnp.float32),
        ],
        axis=0,
    )
    ext[:, LANES:] = meta.T.astype(jnp.bfloat16)
    loads[3].wait()

    def side_copy(side, source, landing, send, recv):
        return pltpu.make_async_remote_copy(
            src_ref=source,
            dst_ref=landing,
            send_sem=send.at[side],
            recv_sem=recv.at[side],
            device_id={"lon": me - 1 if side == 0 else me + 1},
            device_id_type=pl.DeviceIdType.MESH,
        )

    exists = (me > 0, me < tiles - 1)

    def cel_copy(side):
        source = cel_hbm.at[pl.ds(0 if side == 0 else rows - RIM, RIM)]
        landing = kappa_ref.at[pl.ds(RIM + rows if side == 0 else 0, RIM)]
        return side_copy(side, source, landing, cel_send.at[0], cel_recv.at[0])

    def rim_copy(side, n):
        return side_copy(
            side, rim_out.at[side, n], rim_in.at[side, n], rim_send.at[n], rim_recv.at[n]
        )

    def obs_copy(code):
        return pltpu.make_async_remote_copy(
            src_ref=sent.at[code],
            dst_ref=got.at[code],
            send_sem=send_sem.at[code],
            recv_sem=recv_sem.at[code],
            device_id={"lon": partner(code)},
            device_id_type=pl.DeviceIdType.MESH,
        )

    def pack(code, there, box):
        slot_hot = placed[...] == there * cap + iota((cap, stations), 0)
        matrix = jnp.where(slot_hot, 1.0, 0.0).astype(jnp.bfloat16)
        packed = jnp.dot(matrix, ext[...], preferred_element_type=jnp.float32)
        box[code, :cap, :] = packed[:, :LANES].astype(jnp.bfloat16)
        turned = packed[:, LANES:].T
        for n in range(pages):
            box[code, cap + n * META : cap + (n + 1) * META, :page] = turned[
                :META, n * page : (n + 1) * page
            ].astype(jnp.bfloat16)

    def pack_and_send(turn, carry):
        code = order(turn, tiles)
        pack(code, partner(code), sent)
        obs_copy(code).start()
        return carry

    pack(tiles // 2, partner(tiles // 2), sent)
    pl.semaphore_wait(barrier, tiles - 1)
    for side in range(2):

        @pl.when(exists[side])
        def _():
            cel_copy(side).start()

    obs_copy(tiles // 2).start()
    lax.fori_loop(1, tiles - 1, pack_and_send, 0)
    pack(0, me, got)

    def weigh(code):
        sheets = [
            got[code, cap + n * META : cap + (n + 1) * META, :][:, :page].astype(jnp.float32)
            for n in range(pages)
        ]
        meta = sheets[0] if pages == 1 else jnp.concatenate(sheets, axis=1)
        key = meta[steps + 1 : steps + 2] * rows + meta[steps : steps + 1]
        return key.astype(jnp.int32) == iota((rows * chunks, cap), 0), meta

    def spread(code, first):
        near, far = weigh(code), weigh(code + 1)
        for moment in range(steps):
            summed = None
            for n, (hot, meta) in enumerate((near, far)):
                weighted = jnp.where(hot, meta[moment : moment + 1], 0.0).astype(jnp.bfloat16)
                term = jnp.dot(
                    weighted, got[code + n, :cap, :], preferred_element_type=jnp.float32
                )
                summed = term if summed is None else summed + term
            for c in range(chunks):
                cells = (moment, own, slice(c * LANES, (c + 1) * LANES))
                piece = summed[c * rows : (c + 1) * rows]
                field[cells] = piece if first else field[cells] + piece

    for load in loads[4:]:
        load.wait()
    for side in range(2):
        rim = slice(RIM + rows, wide) if side == 0 else slice(0, RIM)

        @pl.when(exists[1 - side])
        def _():
            cel_copy(side).wait_recv()

        @pl.when(jnp.logical_not(exists[1 - side]))
        def _():
            kappa_ref[rim] = jnp.zeros((RIM, lat), jnp.float32)
            field[:, rim] = jnp.zeros((steps, RIM, lat), jnp.float32)

    kappa = kappa_ref[...]
    column = iota((wide, lat), 1)
    north = 0.5 * (kappa + pltpu.roll(kappa, 1, 0))
    south = 0.5 * (kappa + pltpu.roll(kappa, wide - 1, 0))
    west_edge, east_edge = column == 0, column == lat - 1
    west = 0.5 * (kappa + jnp.where(west_edge, 0.0, pltpu.roll(kappa, 1, 1)))
    east = 0.5 * (kappa + jnp.where(east_edge, 0.0, pltpu.roll(kappa, lat - 1, 1)))
    coef[0] = 2.0 - (north + south + west + east)
    coef[1] = north
    coef[2] = south
    coef[3] = jnp.where(west_edge, 0.0, west)
    coef[4] = jnp.where(east_edge, 0.0, east)

    moment = lax.div(iota((steps * LANES, LANES), 0), LANES).astype(jnp.float32)
    window = iota((steps * LANES, LANES), 1)
    tent_at = lax.rem(window, NWIN).astype(jnp.float32) * (steps - 1) / (NWIN - 1)
    tent = jnp.maximum(0.0, 1.0 - jnp.abs(moment - tent_at))
    for rake in range(2):
        basis[rake] = jnp.where(lax.div(window, NWIN) == rake, tent, 0.0)

    obs_copy(1).wait_recv()
    spread(0, True)

    def receive(pair, carry):
        obs_copy(2 * pair).wait_recv()
        obs_copy(2 * pair + 1).wait_recv()
        spread(2 * pair, False)
        return carry

    lax.fori_loop(1, tiles // 2, receive, 0)

    last = steps - 1
    level = iota((RIM, lat), 0)
    for n in range(steps // 2):
        t = last - n
        head, tail = field[t, own][:RIM], field[last - t, own][:RIM]
        rim_out[0, n] = jnp.where(level < t, head, pltpu.roll(tail, t, 0))
        head, tail = field[t, own][rows - RIM :], field[last - t, own][rows - RIM :]
        rim_out[1, n] = jnp.where(level >= RIM - t, head, pltpu.roll(tail, RIM - t, 0))
        for side in range(2):

            @pl.when(exists[side])
            def _():
                rim_copy(side, n).start()

    def land(n):
        t = last - n
        for side in range(2):

            @pl.when(exists[1 - side])
            def _():
                rim_copy(side, n).wait_recv()
                tile = rim_in[side, n]
                if side == 0:
                    rim = slice(RIM + rows, wide)
                    field[t, rim] = jnp.where(level < t, tile, 0.0)
                    field[last - t, rim] = jnp.where(
                        level < last - t, pltpu.roll(tile, RIM - t, 0), 0.0
                    )
                else:
                    rim = slice(0, RIM)
                    field[t, rim] = jnp.where(level >= RIM - t, tile, 0.0)
                    field[last - t, rim] = jnp.where(level > t, pltpu.roll(tile, t, 0), 0.0)

    line = iota((wide, lat), 0) + (me * rows - RIM)
    inside = jnp.logical_and(line >= 0, line < tiles * rows)

    def keep(t, surface):
        for c in range(chunks):
            past[t, c] = surface[own, c * LANES : (c + 1) * LANES]

    def advance(step, carry):
        t = last - step
        current = field[t + 1]
        moved = (
            coef[0] * current
            + coef[1] * pltpu.roll(current, 1, 0)
            + coef[2] * pltpu.roll(current, wide - 1, 0)
            + coef[3] * pltpu.roll(current, 1, 1)
            + coef[4] * pltpu.roll(current, lat - 1, 1)
            + field[t]
        )
        if not isinstance(step, int) or step > 1:
            moved = moved - field[t + 2]
        fresh = jnp.where(inside, moved, 0.0)
        field[t] = fresh
        keep(t, fresh)
        return carry

    land(0)
    keep(last, field[last])
    for n in range(1, steps // 2):
        land(n)
        advance(n, 0)
    lax.fori_loop(steps // 2, steps, advance, 0)
    store = pltpu.make_async_copy(field.at[0, pl.ds(RIM, rows)], out_ref, load_sem.at[len(loads)])
    store.start()

    def pick(segment, carry):
        block = segb_ref[segment]
        line, chunk = lax.div(block, chunks), lax.rem(block, chunks)
        for t in range(steps):
            picks[t, pl.ds(segment, 1)] = past[t, chunk, pl.ds(line, 1)]
        return carry

    lax.fori_loop(0, segments, pick, 0)

    lines = tiles * 8
    number = iota((lines, segments), 0)
    fault = jnp.where(
        lax.rem(number, 8) < SUB_DEV, lax.div(number, 8) * SUB_DEV + lax.rem(number, 8), -1
    )
    owner_hot = jnp.where(segf_ref[...] == fault, 1.0, 0.0)
    green = green_ref[...].astype(jnp.float32)
    total = None
    for rake in range(2):
        weights = green[:, rake * LANES : (rake + 1) * LANES]
        products = jnp.concatenate([picks[t] * weights for t in range(steps)], axis=1)
        by_fault = jnp.dot(owner_hot, products, precision=HIGH, preferred_element_type=jnp.float32)
        term = jnp.dot(by_fault, basis[rake], precision=HIGH, preferred_element_type=jnp.float32)
        total = term if total is None else total + term
    part_out[...] = total.reshape(tiles, 8, LANES)

    def part_copy(code):
        there = partner(code)
        return pltpu.make_async_remote_copy(
            src_ref=part_out.at[there],
            dst_ref=part_in.at[code],
            send_sem=part_send.at[code],
            recv_sem=part_recv.at[code],
            device_id={"lon": there},
            device_id_type=pl.DeviceIdType.MESH,
        )

    others(lambda code: part_copy(code).start())
    part_in[0] = part_out[me]

    others(lambda code: obs_copy(code).wait_send())
    for side in range(2):

        @pl.when(exists[side])
        def _():
            cel_copy(side).wait_send()
            for n in range(steps // 2):
                rim_copy(side, n).wait_send()

    others(lambda code: part_copy(code).wait())
    store.wait()
    grad_ref[...] = jnp.sum(part_in[...], axis=0)[:SUB_DEV, : 2 * NWIN]


def local(
    celerity,
    station_tile,
    station_block,
    footprint,
    misfit,
    segment_block,
    segment_fault,
    green_uplift,
):
    tiles = lax.axis_size("lon")
    rows, lat = celerity.shape
    stations = footprint.shape[0]
    steps = misfit.shape[0]
    segments = green_uplift.shape[0]
    cap = 2 * stations // tiles
    depth = cap + META * -(-cap // LANES)
    dma = pltpu.SemaphoreType.DMA
    vmem = pl.BlockSpec(memory_space=pltpu.VMEM)
    return pl.pallas_call(
        functools.partial(kernel, tiles, cap),
        out_shape=(
            jax.ShapeDtypeStruct((rows, lat), jnp.float32),
            jax.ShapeDtypeStruct((SUB_DEV, 2 * NWIN), jnp.float32),
        ),
        in_specs=[pl.BlockSpec(memory_space=pltpu.HBM)] * 8,
        out_specs=(pl.BlockSpec(memory_space=pltpu.HBM), vmem),
        scratch_shapes=[
            pltpu.VMEM((1, stations), jnp.int32),
            pltpu.VMEM((1, stations), jnp.int32),
            pltpu.VMEM((steps, stations), jnp.bfloat16),
            pltpu.SMEM((segments,), jnp.int32),
            pltpu.VMEM((1, segments), jnp.int32),
            pltpu.VMEM((segments, 2 * LANES), jnp.bfloat16),
            pltpu.VMEM((rows + 2 * RIM, lat), jnp.float32),
            pltpu.VMEM((5, rows + 2 * RIM, lat), jnp.float32),
            pltpu.VMEM((2, steps * LANES, LANES), jnp.float32),
            dma((9,)),
            pltpu.VMEM((stations, 2 * LANES), jnp.bfloat16),
            pltpu.VMEM((1, stations), jnp.int32),
            pltpu.VMEM((tiles, depth, LANES), jnp.bfloat16),
            pltpu.VMEM((tiles, depth, LANES), jnp.bfloat16),
            pltpu.VMEM((steps, rows + 2 * RIM, lat), jnp.float32),
            pltpu.VMEM((2, steps // 2, RIM, lat), jnp.float32),
            pltpu.VMEM((2, steps // 2, RIM, lat), jnp.float32),
            pltpu.VMEM((steps, lat // LANES, rows, LANES), jnp.float32),
            pltpu.VMEM((steps, segments, LANES), jnp.float32),
            pltpu.VMEM((tiles, 8, LANES), jnp.float32),
            pltpu.VMEM((tiles, 8, LANES), jnp.float32),
            dma((tiles,)),
            dma((tiles,)),
            dma((steps // 2, 2)),
            dma((steps // 2, 2)),
            dma((1, 2)),
            dma((1, 2)),
            dma((tiles,)),
            dma((tiles,)),
        ],
        compiler_params=pltpu.CompilerParams(
            collective_id=0, has_side_effects=True, vmem_limit_bytes=64 * 1024 * 1024
        ),
    )(
        celerity,
        station_tile.reshape(1, stations),
        station_block.reshape(1, stations),
        footprint,
        misfit,
        segment_block,
        segment_fault.reshape(1, segments),
        green_uplift,
    )


def solution(mesh):
    placed = (
        P("lon", None),
        P(("groups", "lon"), None),
        P(("groups", "lon")),
        P(("groups", "lon"), None),
        P(None, ("groups", "lon")),
        P("lon"),
        P("lon"),
        P("lon", None),
    )
    return jax.shard_map(
        local,
        mesh=mesh,
        in_specs=placed,
        out_specs=(P(("groups", "lon"), None), P(("groups", "lon"), None)),
        check_vma=False,
    )
```
